32 devices in a mesh: mem: 8 (over z, x), pb: 4 (over y, core).
Axes of the slice: x: 2, y: 2, z: 4, core: 2. Of those that a mesh axis runs over, the one named last changes fastest.
Arguments:
- query_raw: bfloat16 [1024, 5120], P('mem', 'pb'), may hold values from -420 to 420
- query_tangent: bfloat16 [1024, 5120], P('mem', 'pb'), may hold values from -6 to 6
- norm_gain: float32 [5120], P('pb'), may hold values from 0.1 to 1.9
- mem_keys: bfloat16 [4096, 5120], P('mem', 'pb'), may hold values from -110 to 110
- mem_values: bfloat16 [4096, 5120], P('mem', 'pb'), may hold values from -6 to 6
- retrieved: int32 [256, 4], P('mem'), may hold values from 0 to 7, all different within a row; in each aligned block of 32 rows (0 to 31, 32 to 63, ...) at most 32 rows name the same one
Outputs:
- attended: bfloat16 [1024, 5120], P('mem', 'pb')
- attended_tangent: bfloat16 [1024, 5120], P('mem', 'pb')
The draws below stay inside these ranges and needn't reach their ends.
Inputs may be any that keep to these rules, and one draw needn't show every extreme that they name: `retrieved`: each row names 4 different frames; among the 32 rows of one index of mem no frame is named by more than 32 rows, a bound that some block reaches of them.
All inputs are finite; a program needn't handle non-finite values.
Results may differ from the reference program's by a relative error of at most 0.0055.
The reference program's roundings to bfloat16 on the way count: a program that leaves them out, or rounds other values in their place, can miss the bound.
Values may be sent and summed in bfloat16 or wider, within the bound.
A program may use at most 64 MiB of HBM per device.

```python
import math
import jax
import jax.numpy as jnp
import numpy as np
from jax import lax

HEADS = 40
HDIM = 128
FRAME = 512
QBLK = 4
PICKS = 4
QB_DEV = 32
DIM = 5120
CAP = 32
NFRAMES = 8
MEMTOK = 4096
QBLOCKS = 256
TOKENS = 1024


def draw_query_raw(key, part):
    key = jax.random.fold_in(key, 11)
    base_key = jax.random.fold_in(key, 0)
    column_key = jax.random.fold_in(key, 2)
    row_key = jax.random.fold_in(key, 3)
    positions = jnp.arange(DIM, dtype=jnp.float32) / max(DIM - 1, 1)
    base_draw = jnp.clip(jax.random.normal(base_key, (TOKENS, DIM), jnp.float32), -4.0, 4.0)
    ramp_scale = jnp.exp(0.5 * math.log(3.0) * positions)
    column_scale = ramp_scale * jnp.exp(jax.random.uniform(column_key, (DIM,), jnp.float32, 0.0, math.log(5.8)))
    row_scale = jnp.exp(jax.random.uniform(row_key, (TOKENS, 1), jnp.float32, 0.0, math.log(10.0)))
    return (base_draw * column_scale[None, :] * row_scale).astype(jnp.bfloat16)


def draw_mem_keys(key, part):
    key = jax.random.fold_in(key, 23)
    base_key = jax.random.fold_in(key, 0)
    base_draw = jnp.clip(jax.random.normal(base_key, (MEMTOK, DIM), jnp.float32), -4.0, 4.0)
    return base_draw.astype(jnp.bfloat16)


def block_scale(key, shape, pieces, low, high):
    gain = 1.0
    for axis_at, parts in pieces:
        draws = jax.random.uniform(jax.random.fold_in(jax.random.fold_in(key, 6), axis_at), (parts,), jnp.float32, low / len(pieces), high / len(pieces))
        gain = gain * jnp.repeat(jnp.exp(draws), shape[axis_at] // parts).reshape((-1,) + (1,) * (len(shape) - 1 - axis_at))
    return gain


def shared_out(rng, own, number, rows, count, top, bound, lean):
    order = jax.random.permutation(rng, count)
    crowded, common = shares(count, rows * top, bound, lean, True), shares(count, rows * top, bound, lean, False)
    places = jnp.arange(count)

    def named(sizes, offset_by):
        used = int((sizes > 0).sum())
        fixed = max(1, used // 4)
        shifted = fixed + (places - fixed + offset_by * (used - fixed)) % max(1, count - fixed)
        return jnp.zeros((count,), jnp.int32).at[order[jnp.where(places < fixed, places, shifted)]].set(jnp.asarray(sizes, jnp.int32))

    sizes = jnp.where(number % 4 == 0, named(crowded, number // 4), named(common, number - number // 4 - 1))
    mixed = jax.random.permutation(jax.random.fold_in(own, 3), count)
    donor, taker = mixed[0:count // 2 * 2:2], mixed[1:count // 2 * 2:2]
    margin = jnp.minimum(sizes[donor] - 1, bound - sizes[taker]) // 2
    margin = jnp.where((donor == order[0]) | (taker == order[0]) | (sizes[taker] == 0), 0, jnp.maximum(margin, 0))
    shifted = jax.random.randint(jax.random.fold_in(own, 4), (count // 2,), 0, 1 << 20) % (margin + 1)
    sizes = sizes.at[donor].add(-shifted).at[taker].add(shifted)
    labels = jnp.searchsorted(jnp.cumsum(sizes), jnp.arange(rows * top), side="right").astype(jnp.int32)
    grid = labels.reshape(top, rows).T
    grid = grid[jax.random.permutation(jax.random.fold_in(own, 1), rows)]
    offset_by = jax.random.randint(jax.random.fold_in(own, 2), (rows, 1), 0, top)
    return jnp.take_along_axis(grid, (jnp.arange(top)[None, :] + offset_by) % top, axis=1)


def shares(count, total, bound, lean, full):
    weights = [(1 << 20) // math.isqrt(standing ** lean) + 1 for standing in range(1, count + 1)]
    largest = bound if full else min(bound, max(-(-total // count), total * weights[0] // sum(weights)))
    least = 1 if total - largest >= count - 1 else 0
    counts, rest = [largest] + [least] * (count - 1), total - largest - least * (count - 1)
    while rest > 0:
        candidates = [i for i in range(1, count) if counts[i] < largest] or [i for i in range(1, count) if counts[i] < bound]
        mass, left = sum([weights[i] for i in candidates]), rest
        for i in candidates:
            more = min(bound - counts[i], max(1, left * weights[i] // mass), rest)
            counts[i] = counts[i] + more
            rest = rest - more
    return np.array(counts)


def noise(key, dims, width, most, cuts=(), held_as=jnp.bfloat16):
    level = block_scale(key, dims, cuts, -0.22, 0.18) if cuts else 1.0
    drawn = jax.random.normal(key, dims, jnp.float32) * width * level
    return jnp.minimum(jnp.maximum(drawn, -most), most).astype(held_as)


def setup_inputs(seed: int = 0) -> dict:
    seeds = jax.random.split(jax.random.key(seed), 7)
    query_raw = draw_query_raw(jax.random.fold_in(seeds[6], 71), 0)
    query_tangent = noise(seeds[1], (TOKENS, DIM), 1.0, 6.0, ((0, 8), (1, 4)))
    norm_gain = jnp.clip(1.0 + 0.18 * jax.random.normal(seeds[2], (DIM,), jnp.float32), 0.1, 1.9)
    mem_keys = draw_mem_keys(jax.random.fold_in(seeds[6], 71), 0)
    mem_values = noise(seeds[4], (MEMTOK, DIM), 1.0, 6.0, ((0, 8), (1, 4)))
    retrieved_keys = jax.random.split(jax.random.fold_in(seeds[5], 1), QBLOCKS // QB_DEV)
    retrieved_turns = jax.random.permutation(jax.random.fold_in(seeds[5], 3), QBLOCKS // QB_DEV)
    retrieved = jax.vmap(lambda own, number: shared_out(jax.random.fold_in(seeds[5], 2), own, number, QB_DEV, NFRAMES, PICKS, CAP, 2))(retrieved_keys, retrieved_turns).reshape((QBLOCKS, PICKS))
    return {"query_raw": query_raw, "query_tangent": query_tangent, "norm_gain": norm_gain, "mem_keys": mem_keys, "mem_values": mem_values, "retrieved": retrieved}


EPSILON = 1e-06

def normalize(query_raw, query_tangent, norm_gain):
    values_f = query_raw.astype(jnp.float32)
    tangent_f = query_tangent.astype(jnp.float32)
    feature_count = values_f.shape[1]
    mean_square = lax.optimization_barrier(jnp.sum(values_f * values_f, axis=1, keepdims=True)) / feature_count
    cross_mean = lax.optimization_barrier(jnp.sum(values_f * tangent_f, axis=1, keepdims=True)) / feature_count
    inverse = lax.rsqrt(mean_square + EPSILON)
    normed = (values_f * inverse * norm_gain).astype(jnp.bfloat16)
    normed_tangent = (norm_gain * (tangent_f * inverse - values_f * (inverse ** 3 * cross_mean))).astype(jnp.bfloat16)
    return (normed, normed_tangent)

def round_trip(array):
    return lax.optimization_barrier(array.astype(jnp.bfloat16)).astype(jnp.float32)

def frame_partials(block_query, block_tangent, frame_keys, frame_values):
    score_scale = 1.0 / math.sqrt(HDIM)
    query_f = block_query.astype(jnp.float32)
    tangent_f = block_tangent.astype(jnp.float32)
    keys_f = frame_keys.astype(jnp.float32)
    values_f = frame_values.astype(jnp.float32)
    scores = jnp.einsum('qhd,khd->hqk', query_f, keys_f) * score_scale
    dscores = jnp.einsum('qhd,khd->hqk', tangent_f, keys_f) * score_scale
    peak = lax.optimization_barrier(jnp.max(scores, axis=2))
    weights = jnp.exp(scores - peak[:, :, None])
    total = lax.optimization_barrier(jnp.sum(weights, axis=2))
    drift = weights * dscores
    drift_total = lax.optimization_barrier(jnp.sum(drift, axis=2))
    partial_out = jnp.einsum('hqk,khd->qhd', round_trip(weights), values_f).astype(jnp.bfloat16)
    partial_tangent = jnp.einsum('hqk,khd->qhd', round_trip(drift), values_f).astype(jnp.bfloat16)
    return (partial_out, partial_tangent, peak, total, drift_total)

def merge_picks(partial_out, partial_tangent, peaks, totals, drifts):
    top = lax.optimization_barrier(jnp.max(peaks, axis=0))
    factor = jnp.exp(peaks - top[None])
    merged_total = lax.optimization_barrier(jnp.sum(factor * totals, axis=0))
    merged_drift = lax.optimization_barrier(jnp.sum(factor * drifts, axis=0))
    weight = jnp.transpose(factor, (0, 2, 1))[..., None]
    merged = lax.optimization_barrier(jnp.sum(weight * partial_out.astype(jnp.float32), axis=0))
    merged_tangent = lax.optimization_barrier(jnp.sum(weight * partial_tangent.astype(jnp.float32), axis=0))
    total_t = jnp.transpose(merged_total)[..., None]
    drift_t = jnp.transpose(merged_drift)[..., None]
    attended = merged / total_t
    attended_tangent = merged_tangent / total_t - drift_t / total_t * attended
    return (attended.astype(jnp.bfloat16).reshape(QBLK, DIM), attended_tangent.astype(jnp.bfloat16).reshape(QBLK, DIM))

def reference(query_raw, query_tangent, norm_gain, mem_keys, mem_values, retrieved):
    normed, normed_tangent = normalize(query_raw, query_tangent, norm_gain)
    group_size = math.gcd(QBLOCKS, 8)
    group_count = QBLOCKS // group_size
    query_groups = normed.reshape(group_count, group_size, QBLK, HEADS, HDIM)
    tangent_groups = normed_tangent.reshape(group_count, group_size, QBLK, HEADS, HDIM)
    id_groups = retrieved.reshape(group_count, group_size, PICKS)

    def one_block(block_query, block_tangent, frame_ids):

        def per_pick(frame_id):
            start = (frame_id * FRAME).astype(jnp.int32)
            frame_keys = lax.dynamic_slice_in_dim(mem_keys, start, FRAME, 0).reshape(FRAME, HEADS, HDIM)
            frame_values = lax.dynamic_slice_in_dim(mem_values, start, FRAME, 0).reshape(FRAME, HEADS, HDIM)
            return frame_partials(block_query, block_tangent, frame_keys, frame_values)
        return merge_picks(*jax.vmap(per_pick)(frame_ids))

    def one_group(group):
        return jax.vmap(one_block)(group[0], group[1], group[2])
    attended, attended_tangent = lax.map(one_group, (query_groups, tangent_groups, id_groups))
    return (attended.reshape(TOKENS, DIM), attended_tangent.reshape(TOKENS, DIM))
```

```python
import functools
import math

import jax
import jax.numpy as jnp
from jax import lax
from jax.experimental import pallas as pl
from jax.experimental.pallas import tpu as pltpu
from jax.sharding import PartitionSpec as P

HEADS = 40
HDIM = 128
QBLK = 4


EPSILON = 1e-06


def head_partials(query_rows, tangent_rows, mem_keys, mem_values, head_count):
    row_count = query_rows.shape[0]
    score_scale = 1.0 / math.sqrt(HDIM)
    feature_width = head_count * HDIM
    dims_spec = (((1,), (1,)), ((), ()))

    def head_step(head_index, carry):
        start = head_index * HDIM
        query_head = lax.dynamic_slice_in_dim(query_rows, start, HDIM, 1)
        key_head = lax.dynamic_slice_in_dim(mem_keys, start, HDIM, 1)
        value_head = lax.dynamic_slice_in_dim(mem_values, start, HDIM, 1)
        scores = (
            lax.dot_general(query_head, key_head, dims_spec, preferred_element_type=jnp.float32)
            * score_scale
        )
        peak = jnp.max(scores, axis=1)
        weights = jnp.exp(scores - peak[:, None])
        updated = list(carry)
        total = jnp.sum(weights, axis=1)
        out_head = jnp.dot(
            weights.astype(jnp.bfloat16), value_head, preferred_element_type=jnp.float32
        ).astype(jnp.bfloat16)
        updated[0] = lax.dynamic_update_slice_in_dim(carry[0], out_head, start, 1)
        updated[1] = lax.dynamic_update_slice_in_dim(carry[1], peak[:, None], head_index, 1)
        updated[2] = lax.dynamic_update_slice_in_dim(carry[2], total[:, None], head_index, 1)
        tangent_head = lax.dynamic_slice_in_dim(tangent_rows, start, HDIM, 1)
        dscores = (
            lax.dot_general(tangent_head, key_head, dims_spec, preferred_element_type=jnp.float32)
            * score_scale
        )
        drift = weights * dscores
        drift_total = jnp.sum(drift, axis=1)
        tangent_out = jnp.dot(
            drift.astype(jnp.bfloat16), value_head, preferred_element_type=jnp.float32
        ).astype(jnp.bfloat16)
        updated[3] = lax.dynamic_update_slice_in_dim(carry[3], tangent_out, start, 1)
        updated[4] = lax.dynamic_update_slice_in_dim(carry[4], drift_total[:, None], head_index, 1)
        return tuple(updated)

    stat_zeros = jnp.zeros((row_count, head_count), jnp.float32)
    wide_zeros = jnp.zeros((row_count, feature_width), jnp.bfloat16)
    initial = (wide_zeros, stat_zeros, stat_zeros, wide_zeros, stat_zeros)
    return lax.fori_loop(0, head_count, head_step, initial)


def local(query_raw, query_tangent, norm_gain, mem_keys, mem_values, retrieved):
    owners = lax.axis_size("mem")
    block_count, pick_count = retrieved.shape
    token_count, feature_width = query_raw.shape
    head_count = feature_width // HDIM
    capacity = max(2, 2 * block_count * pick_count // owners)
    values_f = query_raw.astype(jnp.float32)
    tangent_f = query_tangent.astype(jnp.float32)
    square_sum, cross_sum = lax.psum(
        (jnp.sum(values_f * values_f, axis=1), jnp.sum(values_f * tangent_f, axis=1)), "pb"
    )
    full_width = HEADS * HDIM
    inverse = lax.rsqrt(square_sum / full_width + EPSILON)[:, None]
    cross_mean = (cross_sum / full_width)[:, None]
    normed = (values_f * inverse * norm_gain).astype(jnp.bfloat16)
    normed_tangent = (
        norm_gain * (tangent_f * inverse - values_f * (inverse**3 * cross_mean))
    ).astype(jnp.bfloat16)
    flat_ids = retrieved.reshape(-1)
    one_hot = (flat_ids[:, None] == jnp.arange(owners, dtype=jnp.int32)[None, :]).astype(jnp.int32)
    earlier = jnp.cumsum(one_hot, axis=0) - one_hot
    position = jnp.sum(earlier * one_hot, axis=1)
    target = flat_ids * capacity + position

    def pack(rows_in):
        copies = jnp.repeat(rows_in.reshape(block_count, QBLK, feature_width), pick_count, axis=0)
        buffer_rows = (
            jnp.zeros((owners * capacity, QBLK, feature_width), jnp.bfloat16).at[target].set(copies)
        )
        return buffer_rows.reshape(owners, capacity * QBLK, feature_width)

    send_query = pack(normed)
    send_tangent = pack(normed_tangent)

    def flatten(piece):
        return piece.reshape(-1, piece.shape[-1])

    def unflatten(array, sources, slot_rows):
        return array.reshape(sources, slot_rows, array.shape[-1])

    pieces = (
        lax.all_to_all(send_query, "mem", split_axis=0, concat_axis=0, tiled=True),
        lax.all_to_all(send_tangent, "mem", split_axis=0, concat_axis=0, tiled=True),
    )
    sources, slot_rows, _unused = pieces[0].shape
    out_part, peak_part, total_part, tangent_part, drift_part = head_partials(
        flatten(pieces[0]), flatten(pieces[1]), mem_keys, mem_values, head_count
    )
    partial_out = lax.all_to_all(
        unflatten(out_part, sources, slot_rows).astype(jnp.float32),
        "mem",
        split_axis=0,
        concat_axis=0,
        tiled=True,
    ).astype(jnp.bfloat16)
    peaks = lax.all_to_all(
        unflatten(peak_part, sources, slot_rows), "mem", split_axis=0, concat_axis=0, tiled=True
    )
    totals = lax.all_to_all(
        unflatten(total_part, sources, slot_rows), "mem", split_axis=0, concat_axis=0, tiled=True
    )
    partial_tangent = lax.all_to_all(
        unflatten(tangent_part, sources, slot_rows).astype(jnp.float32),
        "mem",
        split_axis=0,
        concat_axis=0,
        tiled=True,
    ).astype(jnp.bfloat16)
    drifts = lax.all_to_all(
        unflatten(drift_part, sources, slot_rows), "mem", split_axis=0, concat_axis=0, tiled=True
    )

    def pick_rows(array, trailing):
        slots = array.reshape((owners * capacity, QBLK) + trailing)
        return slots[target].reshape((block_count, pick_count, QBLK) + trailing)

    out_picked = pick_rows(partial_out, (head_count, HDIM))
    tangent_picked = pick_rows(partial_tangent, (head_count, HDIM))
    peak_picked = pick_rows(peaks, (head_count,))
    total_picked = pick_rows(totals, (head_count,))
    drift_picked = pick_rows(drifts, (head_count,))
    top = jnp.max(peak_picked, axis=1)
    factor = jnp.exp(peak_picked - top[:, None])
    merged_total = jnp.sum(factor * total_picked, axis=1)[..., None]
    merged_drift = jnp.sum(factor * drift_picked, axis=1)[..., None]
    merged = jnp.sum(factor[..., None] * out_picked.astype(jnp.float32), axis=1)
    merged_tangent = jnp.sum(factor[..., None] * tangent_picked.astype(jnp.float32), axis=1)
    attended = merged / merged_total
    attended_tangent = merged_tangent / merged_total - merged_drift / merged_total * attended
    return (
        attended.astype(jnp.bfloat16).reshape(token_count, feature_width),
        attended_tangent.astype(jnp.bfloat16).reshape(token_count, feature_width),
    )

LINE = 4
NEG = -1e30
MESH = pl.DeviceIdType.MESH
NT = (((1,), (1,)), ((), ()))


def fused_kernel(
    heads,
    shares,
    full_width,
    raw_ref,
    tan_ref,
    gain_ref,
    keys_ref,
    vals_ref,
    picked_ref,
    out_ref,
    dout_ref,
    kv_in,
    norm_out,
    norm_in,
    pick_all,
    q_all,
    part_out,
    part_in,
    stat_out,
    stat_in,
    own_part,
    own_stat,
    kv_send,
    kv_recv,
    norm_send,
    norm_recv,
    pick_send,
    pick_recv,
    q_send,
    q_recv,
    part_send,
    part_recv,
    stat_send,
    stat_recv,
):
    me = lax.axis_index("mem")
    share = lax.axis_index("pb")
    pos, side = me // 2, lax.rem(me, 2)
    rows = raw_ref.shape[0]
    scale = 1.0 / math.sqrt(HDIM)

    def mem_of(position):
        return position * 2 + side

    other_side = pos * 2 + (1 - side)
    far = [lax.rem(pos + j, LINE) for j in range(1, LINE)]
    shares_far = [lax.rem(share + j, shares) for j in range(1, shares)]

    def cols(head):
        return pl.ds(pl.multiple_of(head * HDIM, HDIM), HDIM)

    barrier = pltpu.get_barrier_semaphore()
    pl.semaphore_signal(
        barrier, inc=1, device_id={"mem": other_side, "pb": share}, device_id_type=MESH
    )
    for place in far:
        pl.semaphore_signal(
            barrier, inc=1, device_id={"mem": mem_of(place), "pb": share}, device_id_type=MESH
        )
    for s in shares_far:
        pl.semaphore_signal(barrier, inc=1, device_id={"mem": me, "pb": s}, device_id_type=MESH)
    pl.semaphore_wait(barrier, 1 + len(far) + len(shares_far))

    def remote(src, dst, send, recv, mem, pb):
        return pltpu.make_async_remote_copy(
            src_ref=src,
            dst_ref=dst,
            send_sem=send,
            recv_sem=recv,
            device_id={"mem": mem, "pb": pb},
            device_id_type=MESH,
        )

    def kv_copy(which, head):
        src = (keys_ref, vals_ref)[which].at[:, cols(head)]
        return remote(
            src,
            kv_in.at[which, head],
            kv_send.at[which, head],
            kv_recv.at[which, head],
            other_side,
            share,
        )

    def norm_copy(slot, to):
        return remote(
            norm_out, norm_in.at[slot], norm_send.at[to], norm_recv.at[slot], me, to
        )

    def pick_copy(slot, to):
        return remote(
            picked_ref,
            pick_all.at[slot],
            pick_send.at[to],
            pick_recv.at[slot],
            mem_of(to),
            share,
        )

    def q_copy(origin, head, way):
        to = lax.rem(pos + (1 if way == 0 else LINE - 1), LINE)
        return remote(
            q_all.at[origin, head],
            q_all.at[origin, head],
            q_send.at[origin, way, head],
            q_recv.at[origin, head],
            mem_of(to),
            share,
        )

    def part_copy(slot, to, head):
        return remote(
            part_out.at[to, head],
            part_in.at[slot, head],
            part_send.at[to, head],
            part_recv.at[slot, head],
            mem_of(to),
            share,
        )

    def stat_copy(slot, to, head):
        return remote(
            stat_out.at[to, head],
            stat_in.at[slot, head],
            stat_send.at[to, head],
            stat_recv.at[slot, head],
            mem_of(to),
            share,
        )

    def add_sums(head, carry):
        square, cross = carry
        raw = raw_ref[:, cols(head)].astype(jnp.float32)
        tan = tan_ref[:, cols(head)].astype(jnp.float32)
        return square + raw * raw, cross + raw * tan

    blank = jnp.zeros((rows, HDIM), jnp.float32)
    square, cross = lax.fori_loop(0, heads, add_sums, (blank, blank))
    lane = lax.broadcasted_iota(jnp.int32, (rows, HDIM), 1)
    sums = jnp.where(
        lane == 0,
        jnp.sum(square, axis=1, keepdims=True),
        jnp.where(lane == 1, jnp.sum(cross, axis=1, keepdims=True), 0.0),
    )
    sums_t = sums.T[0:8, :]
    norm_out[...] = sums_t
    for s in shares_far:
        norm_copy(share, s).start()
    for place in far:
        pick_copy(pos, place).start()

    def start_kv(head, carry):
        kv_copy(0, head).start()
        kv_copy(1, head).start()
        return carry

    lax.fori_loop(0, heads, start_kv, 0)

    for s in shares_far:
        norm_copy(s, s).wait_recv()
        sums_t = sums_t + norm_in[s]
    sums = jnp.concatenate([sums_t] + [jnp.zeros_like(sums_t)] * (HDIM // 8 - 1), axis=0).T
    inverse = lax.rsqrt(sums[:, 0:1] / full_width + EPSILON)
    cross_mean = sums[:, 1:2] / full_width
    slope = inverse**3 * cross_mean

    def normalize(head, carry):
        raw = raw_ref[:, cols(head)].astype(jnp.float32)
        tan = tan_ref[:, cols(head)].astype(jnp.float32)
        gain = gain_ref[:, cols(head)]
        q_all[pos, head, 0:rows, :] = (raw * inverse * gain).astype(jnp.bfloat16)
        q_all[pos, head, rows : 2 * rows, :] = (gain * (tan * inverse - raw * slope)).astype(
            jnp.bfloat16
        )

        @pl.when(pos < LINE - 1)
        def _():
            q_copy(pos, head, 0).start()

        @pl.when(pos > 0)
        def _():
            q_copy(pos, head, 1).start()

        return carry

    lax.fori_loop(0, heads, normalize, 0)

    for place in far:
        pick_copy(place, place).wait_recv()

    def forward(head, hop):
        @pl.when(pos >= hop)
        def _():
            q_copy(pos - hop, head, 0).wait_recv()

            @pl.when(pos < LINE - 1)
            def _():
                q_copy(pos - hop, head, 0).start()

        @pl.when(pos < LINE - hop)
        def _():
            q_copy(pos + hop, head, 1).wait_recv()

            @pl.when(pos > 0)
            def _():
                q_copy(pos + hop, head, 1).start()

    frame_row = lax.broadcasted_iota(jnp.int32, (8, rows), 0)

    def compute(head):
        kv_copy(0, head).wait_recv()
        kv_copy(1, head).wait_recv()
        frames = (
            (me, keys_ref[:, cols(head)], vals_ref[:, cols(head)].T),
            (other_side, kv_in[0, head], kv_in[1, head].T),
        )
        for place in far + [pos]:
            query = q_all[place, head]
            masks = picked_ref[...] if place is pos else pick_all[place]
            got = []
            for frame, keys, vals_t in frames:
                both = lax.dot_general(keys, query, NT, preferred_element_type=jnp.float32) * scale
                score, dscore = both[:, 0:rows], both[:, rows : 2 * rows]
                peak = jnp.max(score, axis=0, keepdims=True)
                weight = jnp.exp(score - peak)
                drift = weight * dscore
                mixed = jnp.concatenate(
                    [weight.astype(jnp.bfloat16), drift.astype(jnp.bfloat16)], axis=1
                )
                part = jnp.dot(vals_t, mixed, preferred_element_type=jnp.float32)
                mask = jnp.sum(jnp.where(frame_row == frame, masks, 0.0), axis=0, keepdims=True)
                got.append(
                    (
                        mask,
                        jnp.where(mask > 0.0, peak, NEG),
                        jnp.sum(weight, axis=0, keepdims=True),
                        jnp.sum(drift, axis=0, keepdims=True),
                        part.astype(jnp.bfloat16).astype(jnp.float32),
                    )
                )
            top = jnp.maximum(got[0][1], got[1][1])
            fs = [jnp.exp(g[1] - top) * g[0] for g in got]
            total = fs[0] * got[0][2] + fs[1] * got[1][2]
            drift_total = fs[0] * got[0][3] + fs[1] * got[1][3]
            merged = fs[0] * got[0][4][:, 0:rows] + fs[1] * got[1][4][:, 0:rows]
            tangent = fs[0] * got[0][4][:, rows:] + fs[1] * got[1][4][:, rows:]
            shift = got[0][0] * got[1][0] * drift_total / jnp.maximum(total, 0.5)
            if place is pos:
                shift = jnp.zeros_like(shift)
            stats = jnp.concatenate(
                [top, total, drift_total, shift, jnp.zeros((4, rows), jnp.float32)], axis=0
            )
            if place is pos:
                own_part[head, :, 0:rows] = merged
                own_part[head, :, rows:] = tangent
                own_stat[head] = stats
            else:
                part_out[place, head, :, 0:rows] = merged.astype(jnp.bfloat16)
                part_out[place, head, :, rows:] = (tangent - shift * merged).astype(jnp.bfloat16)
                stat_out[place, head] = stats
                part_copy(pos, place, head).start()
                stat_copy(pos, place, head).start()

    def merge(head):
        parts, stats = [own_part[head]], [own_stat[head]]
        for place in far:
            part_copy(place, place, head).wait_recv()
            stat_copy(place, place, head).wait_recv()
            parts.append(part_in[place, head].astype(jnp.float32))
            stats.append(stat_in[place, head])
        top = functools.reduce(jnp.maximum, [s[0:1] for s in stats])
        total = drift_total = jnp.zeros_like(top)
        merged = tangent = jnp.zeros((HDIM, rows), jnp.float32)
        for part, stat in zip(parts, stats):
            factor = jnp.exp(stat[0:1] - top)
            total += factor * stat[1:2]
            drift_total += factor * stat[2:3]
            merged += factor * part[:, 0:rows]
            tangent += factor * (part[:, rows:] + stat[3:4] * part[:, 0:rows])
        attended = merged / total
        attended_tangent = tangent / total - drift_total / total * attended
        out_ref[:, cols(head)] = attended.T.astype(jnp.bfloat16)
        dout_ref[:, cols(head)] = attended_tangent.T.astype(jnp.bfloat16)

    lag = 2

    def step(t, carry):
        @pl.when(t < heads)
        def _():
            forward(t, 1)

        @pl.when((t >= 1) & (t < heads + 1))
        def _():
            forward(t - 1, 2)

        @pl.when((t >= 2) & (t < heads + 2))
        def _():
            forward(t - 2, 3)
            compute(t - 2)

        @pl.when(t >= 2 + lag)
        def _():
            merge(t - 2 - lag)

        return carry

    lax.fori_loop(0, heads + 2 + lag, step, 0)

    for s in shares_far:
        norm_copy(share, s).wait_send()
    for place in far:
        pick_copy(pos, place).wait_send()

    def drain(head, carry):
        kv_copy(0, head).wait_send()
        kv_copy(1, head).wait_send()
        for place in far:
            part_copy(pos, place, head).wait_send()
            stat_copy(pos, place, head).wait_send()
        for hop in range(LINE - 1):

            @pl.when((pos >= hop) & (pos < LINE - 1))
            def _():
                q_copy(pos - hop, head, 0).wait_send()

            @pl.when((pos < LINE - hop) & (pos > 0))
            def _():
                q_copy(pos + hop, head, 1).wait_send()

        return carry

    lax.fori_loop(0, heads, drain, 0)


def dense_local(query_raw, query_tangent, norm_gain, mem_keys, mem_values, retrieved):
    shares = lax.axis_size("pb")
    owners = lax.axis_size("mem")
    rows, width = query_raw.shape
    frame = mem_keys.shape[0]
    heads = width // HDIM
    named = jnp.arange(owners, dtype=jnp.int32)[:, None, None] == retrieved[None]
    picked = jnp.repeat(jnp.any(named, axis=2), QBLK, axis=1).astype(jnp.float32)
    vmem = pl.BlockSpec(memory_space=pltpu.VMEM)
    dma = pltpu.SemaphoreType.DMA
    f32, bf16 = jnp.float32, jnp.bfloat16
    return pl.pallas_call(
        functools.partial(fused_kernel, heads, shares, width * shares),
        out_shape=(jax.ShapeDtypeStruct((rows, width), bf16),) * 2,
        in_specs=[vmem] * 6,
        out_specs=(vmem, vmem),
        scratch_shapes=[
            pltpu.VMEM((2, heads, frame, HDIM), bf16),
            pltpu.VMEM((8, rows), f32),
            pltpu.VMEM((shares, 8, rows), f32),
            pltpu.VMEM((LINE, owners, rows), f32),
            pltpu.VMEM((LINE, heads, 2 * rows, HDIM), bf16),
            pltpu.VMEM((LINE, heads, HDIM, 2 * rows), bf16),
            pltpu.VMEM((LINE, heads, HDIM, 2 * rows), bf16),
            pltpu.VMEM((LINE, heads, 8, rows), f32),
            pltpu.VMEM((LINE, heads, 8, rows), f32),
            pltpu.VMEM((heads, HDIM, 2 * rows), f32),
            pltpu.VMEM((heads, 8, rows), f32),
            dma((2, heads)),
            dma((2, heads)),
            dma((shares,)),
            dma((shares,)),
            dma((LINE,)),
            dma((LINE,)),
            dma((LINE, 2, heads)),
            dma((LINE, heads)),
            dma((LINE, heads)),
            dma((LINE, heads)),
            dma((LINE, heads)),
            dma((LINE, heads)),
        ],
        compiler_params=pltpu.CompilerParams(
            collective_id=0, has_side_effects=True, vmem_limit_bytes=48 * 2**20
        ),
    )(query_raw, query_tangent, norm_gain.reshape(1, width), mem_keys, mem_values, picked)


def solution(mesh):
    placed = (
        P("mem", "pb"),
        P("mem", "pb"),
        P("pb"),
        P("mem", "pb"),
        P("mem", "pb"),
        P("mem", None),
    )
    dense = mesh.shape["mem"] == 2 * LINE
    return jax.shard_map(
        dense_local if dense else local,
        mesh=mesh,
        in_specs=placed,
        out_specs=(P("mem", "pb"), P("mem", "pb")),
        check_vma=False,
    )
```

```python
import functools
import math

import jax
import jax.numpy as jnp
from jax import lax
from jax.experimental import pallas as pl
from jax.experimental.pallas import tpu as pltpu
from jax.sharding import PartitionSpec as P

HEADS = 40
HDIM = 128
QBLK = 4


EPSILON = 1e-06


def head_partials(query_rows, tangent_rows, mem_keys, mem_values, head_count):
    row_count = query_rows.shape[0]
    score_scale = 1.0 / math.sqrt(HDIM)
    feature_width = head_count * HDIM
    dims_spec = (((1,), (1,)), ((), ()))

    def head_step(head_index, carry):
        start = head_index * HDIM
        query_head = lax.dynamic_slice_in_dim(query_rows, start, HDIM, 1)
        key_head = lax.dynamic_slice_in_dim(mem_keys, start, HDIM, 1)
        value_head = lax.dynamic_slice_in_dim(mem_values, start, HDIM, 1)
        scores = (
            lax.dot_general(query_head, key_head, dims_spec, preferred_element_type=jnp.float32)
            * score_scale
        )
        peak = jnp.max(scores, axis=1)
        weights = jnp.exp(scores - peak[:, None])
        updated = list(carry)
        total = jnp.sum(weights, axis=1)
        out_head = jnp.dot(
            weights.astype(jnp.bfloat16), value_head, preferred_element_type=jnp.float32
        ).astype(jnp.bfloat16)
        updated[0] = lax.dynamic_update_slice_in_dim(carry[0], out_head, start, 1)
        updated[1] = lax.dynamic_update_slice_in_dim(carry[1], peak[:, None], head_index, 1)
        updated[2] = lax.dynamic_update_slice_in_dim(carry[2], total[:, None], head_index, 1)
        tangent_head = lax.dynamic_slice_in_dim(tangent_rows, start, HDIM, 1)
        dscores = (
            lax.dot_general(tangent_head, key_head, dims_spec, preferred_element_type=jnp.float32)
            * score_scale
        )
        drift = weights * dscores
        drift_total = jnp.sum(drift, axis=1)
        tangent_out = jnp.dot(
            drift.astype(jnp.bfloat16), value_head, preferred_element_type=jnp.float32
        ).astype(jnp.bfloat16)
        updated[3] = lax.dynamic_update_slice_in_dim(carry[3], tangent_out, start, 1)
        updated[4] = lax.dynamic_update_slice_in_dim(carry[4], drift_total[:, None], head_index, 1)
        return tuple(updated)

    stat_zeros = jnp.zeros((row_count, head_count), jnp.float32)
    wide_zeros = jnp.zeros((row_count, feature_width), jnp.bfloat16)
    initial = (wide_zeros, stat_zeros, stat_zeros, wide_zeros, stat_zeros)
    return lax.fori_loop(0, head_count, head_step, initial)


def local(query_raw, query_tangent, norm_gain, mem_keys, mem_values, retrieved):
    owners = lax.axis_size("mem")
    block_count, pick_count = retrieved.shape
    token_count, feature_width = query_raw.shape
    head_count = feature_width // HDIM
    capacity = max(2, 2 * block_count * pick_count // owners)
    values_f = query_raw.astype(jnp.float32)
    tangent_f = query_tangent.astype(jnp.float32)
    square_sum, cross_sum = lax.psum(
        (jnp.sum(values_f * values_f, axis=1), jnp.sum(values_f * tangent_f, axis=1)), "pb"
    )
    full_width = HEADS * HDIM
    inverse = lax.rsqrt(square_sum / full_width + EPSILON)[:, None]
    cross_mean = (cross_sum / full_width)[:, None]
    normed = (values_f * inverse * norm_gain).astype(jnp.bfloat16)
    normed_tangent = (
        norm_gain * (tangent_f * inverse - values_f * (inverse**3 * cross_mean))
    ).astype(jnp.bfloat16)
    flat_ids = retrieved.reshape(-1)
    one_hot = (flat_ids[:, None] == jnp.arange(owners, dtype=jnp.int32)[None, :]).astype(jnp.int32)
    earlier = jnp.cumsum(one_hot, axis=0) - one_hot
    position = jnp.sum(earlier * one_hot, axis=1)
    target = flat_ids * capacity + position

    def pack(rows_in):
        copies = jnp.repeat(rows_in.reshape(block_count, QBLK, feature_width), pick_count, axis=0)
        buffer_rows = (
            jnp.zeros((owners * capacity, QBLK, feature_width), jnp.bfloat16).at[target].set(copies)
        )
        return buffer_rows.reshape(owners, capacity * QBLK, feature_width)

    send_query = pack(normed)
    send_tangent = pack(normed_tangent)

    def flatten(piece):
        return piece.reshape(-1, piece.shape[-1])

    def unflatten(array, sources, slot_rows):
        return array.reshape(sources, slot_rows, array.shape[-1])

    pieces = (
        lax.all_to_all(send_query, "mem", split_axis=0, concat_axis=0, tiled=True),
        lax.all_to_all(send_tangent, "mem", split_axis=0, concat_axis=0, tiled=True),
    )
    sources, slot_rows, _unused = pieces[0].shape
    out_part, peak_part, total_part, tangent_part, drift_part = head_partials(
        flatten(pieces[0]), flatten(pieces[1]), mem_keys, mem_values, head_count
    )
    partial_out = lax.all_to_all(
        unflatten(out_part, sources, slot_rows).astype(jnp.float32),
        "mem",
        split_axis=0,
        concat_axis=0,
        tiled=True,
    ).astype(jnp.bfloat16)
    peaks = lax.all_to_all(
        unflatten(peak_part, sources, slot_rows), "mem", split_axis=0, concat_axis=0, tiled=True
    )
    totals = lax.all_to_all(
        unflatten(total_part, sources, slot_rows), "mem", split_axis=0, concat_axis=0, tiled=True
    )
    partial_tangent = lax.all_to_all(
        unflatten(tangent_part, sources, slot_rows).astype(jnp.float32),
        "mem",
        split_axis=0,
        concat_axis=0,
        tiled=True,
    ).astype(jnp.bfloat16)
    drifts = lax.all_to_all(
        unflatten(drift_part, sources, slot_rows), "mem", split_axis=0, concat_axis=0, tiled=True
    )

    def pick_rows(array, trailing):
        slots = array.reshape((owners * capacity, QBLK) + trailing)
        return slots[target].reshape((block_count, pick_count, QBLK) + trailing)

    out_picked = pick_rows(partial_out, (head_count, HDIM))
    tangent_picked = pick_rows(partial_tangent, (head_count, HDIM))
    peak_picked = pick_rows(peaks, (head_count,))
    total_picked = pick_rows(totals, (head_count,))
    drift_picked = pick_rows(drifts, (head_count,))
    top = jnp.max(peak_picked, axis=1)
    factor = jnp.exp(peak_picked - top[:, None])
    merged_total = jnp.sum(factor * total_picked, axis=1)[..., None]
    merged_drift = jnp.sum(factor * drift_picked, axis=1)[..., None]
    merged = jnp.sum(factor[..., None] * out_picked.astype(jnp.float32), axis=1)
    merged_tangent = jnp.sum(factor[..., None] * tangent_picked.astype(jnp.float32), axis=1)
    attended = merged / merged_total
    attended_tangent = merged_tangent / merged_total - merged_drift / merged_total * attended
    return (
        attended.astype(jnp.bfloat16).reshape(token_count, feature_width),
        attended_tangent.astype(jnp.bfloat16).reshape(token_count, feature_width),
    )

LINE = 4
NEG = -1e30
AHEAD = 4
LEAD = 2
MESH = pl.DeviceIdType.MESH
NT = (((1,), (1,)), ((), ()))


def fused_kernel(
    heads,
    shares,
    full_width,
    raw_ref,
    tan_ref,
    gain_ref,
    keys_ref,
    vals_ref,
    picked_ref,
    out_ref,
    dout_ref,
    kv_in,
    norm_out,
    norm_in,
    pick_all,
    q_all,
    part_out,
    part_in,
    stat_out,
    stat_in,
    own_part,
    own_stat,
    kv_send,
    kv_recv,
    norm_send,
    norm_recv,
    pick_send,
    pick_recv,
    q_send,
    q_recv,
    part_send,
    part_recv,
    stat_send,
    stat_recv,
):
    me = lax.axis_index("mem")
    share = lax.axis_index("pb")
    pos, side = me // 2, lax.rem(me, 2)
    rows = raw_ref.shape[0]
    scale = 1.0 / math.sqrt(HDIM)

    def mem_of(position):
        return position * 2 + side

    other_side = pos * 2 + (1 - side)
    far = [lax.rem(pos + j, LINE) for j in range(1, LINE)]
    shares_far = [lax.rem(share + j, shares) for j in range(1, shares)]

    def cols(head):
        return pl.ds(pl.multiple_of(head * HDIM, HDIM), HDIM)

    barrier = pltpu.get_barrier_semaphore()
    pl.semaphore_signal(
        barrier, inc=1, device_id={"mem": other_side, "pb": share}, device_id_type=MESH
    )
    for place in far:
        pl.semaphore_signal(
            barrier, inc=1, device_id={"mem": mem_of(place), "pb": share}, device_id_type=MESH
        )
    for s in shares_far:
        pl.semaphore_signal(barrier, inc=1, device_id={"mem": me, "pb": s}, device_id_type=MESH)
    pl.semaphore_wait(barrier, 1 + len(far) + len(shares_far))

    def remote(src, dst, send, recv, mem, pb):
        return pltpu.make_async_remote_copy(
            src_ref=src,
            dst_ref=dst,
            send_sem=send,
            recv_sem=recv,
            device_id={"mem": mem, "pb": pb},
            device_id_type=MESH,
        )

    def kv_copy(which, head):
        src = (keys_ref, vals_ref)[which].at[:, cols(head)]
        return remote(
            src,
            kv_in.at[which, head],
            kv_send.at[which, head],
            kv_recv.at[which, head],
            other_side,
            share,
        )

    def norm_copy(slot, to):
        return remote(
            norm_out, norm_in.at[slot], norm_send.at[to], norm_recv.at[slot], me, to
        )

    def pick_copy(slot, to):
        return remote(
            picked_ref,
            pick_all.at[slot],
            pick_send.at[to],
            pick_recv.at[slot],
            mem_of(to),
            share,
        )

    def q_copy(origin, head, way):
        to = lax.rem(pos + (1 if way == 0 else LINE - 1), LINE)
        return remote(
            q_all.at[origin, head],
            q_all.at[origin, head],
            q_send.at[origin, way, head],
            q_recv.at[origin, head],
            mem_of(to),
            share,
        )

    def part_copies(way, dest, head):
        to = mem_of(lax.rem(pos + (1 if way == 0 else LINE - 1), LINE))
        return (
            remote(
                part_out.at[dest, head],
                part_in.at[way, dest, head],
                part_send.at[dest, head],
                part_recv.at[way, dest, head],
                to,
                share,
            ),
            remote(
                stat_out.at[dest, head],
                stat_in.at[way, dest, head],
                stat_send.at[dest, head],
                stat_recv.at[way, dest, head],
                to,
                share,
            ),
        )

    def add_sums(head, carry):
        square, cross = carry
        raw = raw_ref[:, cols(head)].astype(jnp.float32)
        tan = tan_ref[:, cols(head)].astype(jnp.float32)
        return square + raw * raw, cross + raw * tan

    blank = jnp.zeros((rows, HDIM), jnp.float32)
    square, cross = lax.fori_loop(0, heads, add_sums, (blank, blank))
    lane = lax.broadcasted_iota(jnp.int32, (rows, HDIM), 1)
    sums = jnp.where(
        lane == 0,
        jnp.sum(square, axis=1, keepdims=True),
        jnp.where(lane == 1, jnp.sum(cross, axis=1, keepdims=True), 0.0),
    )
    sums_t = sums.T[0:8, :]
    norm_out[...] = sums_t
    for s in shares_far:
        norm_copy(share, s).start()
    for place in far:
        pick_copy(pos, place).start()

    def start_kv(head):
        kv_copy(0, head).start()
        kv_copy(1, head).start()

    stat_row0 = jnp.where(
        lax.broadcasted_iota(jnp.int32, (heads, 8, rows), 1) == 0, 1.0, 0.0
    )
    for head in range(min(AHEAD, heads)):
        start_kv(head)

    @pl.when(pos == 0)
    def _():
        part_in[0, 0] = jnp.zeros_like(part_in[0, 0])
        stat_in[0, 0] = jnp.full_like(stat_in[0, 0], NEG) * stat_row0

    @pl.when(pos == LINE - 1)
    def _():
        part_in[1, LINE - 1] = jnp.zeros_like(part_in[1, LINE - 1])
        stat_in[1, LINE - 1] = jnp.full_like(stat_in[1, LINE - 1], NEG) * stat_row0

    for s in shares_far:
        norm_copy(s, s).wait_recv()
        sums_t = sums_t + norm_in[s]
    sums = jnp.concatenate([sums_t] + [jnp.zeros_like(sums_t)] * (HDIM // 8 - 1), axis=0).T
    inverse = lax.rsqrt(sums[:, 0:1] / full_width + EPSILON)
    cross_mean = sums[:, 1:2] / full_width
    slope = inverse**3 * cross_mean

    def normalize(head, carry):
        raw = raw_ref[:, cols(head)].astype(jnp.float32)
        tan = tan_ref[:, cols(head)].astype(jnp.float32)
        gain = gain_ref[:, cols(head)]
        q_all[pos, head, 0:rows, :] = (raw * inverse * gain).astype(jnp.bfloat16)
        q_all[pos, head, rows : 2 * rows, :] = (gain * (tan * inverse - raw * slope)).astype(
            jnp.bfloat16
        )
        return carry

    def start_q(head):
        @pl.when(pos < LINE - 1)
        def _():
            q_copy(pos, head, 0).start()

        @pl.when(pos > 0)
        def _():
            q_copy(pos, head, 1).start()

    for head in range(min(LEAD, heads)):
        normalize(head, 0)
        start_q(head)
    lax.fori_loop(min(LEAD, heads), heads, normalize, 0)

    for place in far:
        pick_copy(place, place).wait_recv()

    def forward(head, hop):
        @pl.when(pos >= hop)
        def _():
            q_copy(pos - hop, head, 0).wait_recv()

            @pl.when(pos < LINE - 1)
            def _():
                q_copy(pos - hop, head, 0).start()

        @pl.when(pos < LINE - hop)
        def _():
            q_copy(pos + hop, head, 1).wait_recv()

            @pl.when(pos > 0)
            def _():
                q_copy(pos + hop, head, 1).start()

    frame_row = lax.broadcasted_iota(jnp.int32, (8, rows), 0)

    def compute(head):
        kv_copy(0, head).wait_recv()
        kv_copy(1, head).wait_recv()
        frames = (
            (me, keys_ref[:, cols(head)], vals_ref[:, cols(head)].T),
            (other_side, kv_in[0, head], kv_in[1, head].T),
        )
        for place in far + [pos]:
            query = q_all[place, head]
            masks = picked_ref[...] if place is pos else pick_all[place]
            got = []
            for frame, keys, vals_t in frames:
                both = lax.dot_general(keys, query, NT, preferred_element_type=jnp.float32) * scale
                score, dscore = both[:, 0:rows], both[:, rows : 2 * rows]
                peak = jnp.max(score, axis=0, keepdims=True)
                weight = jnp.exp(score - peak)
                drift = weight * dscore
                mixed = jnp.concatenate(
                    [weight.astype(jnp.bfloat16), drift.astype(jnp.bfloat16)], axis=1
                )
                part = jnp.dot(vals_t, mixed, preferred_element_type=jnp.float32)
                mask = jnp.sum(jnp.where(frame_row == frame, masks, 0.0), axis=0, keepdims=True)
                got.append(
                    (
                        mask,
                        jnp.where(mask > 0.0, peak, NEG),
                        jnp.sum(weight, axis=0, keepdims=True),
                        jnp.sum(drift, axis=0, keepdims=True),
                        part.astype(jnp.bfloat16).astype(jnp.float32),
                    )
                )
            top = jnp.maximum(got[0][1], got[1][1])
            fs = [jnp.exp(g[1] - top) * g[0] for g in got]
            total = fs[0] * got[0][2] + fs[1] * got[1][2]
            drift_total = fs[0] * got[0][3] + fs[1] * got[1][3]
            merged = fs[0] * got[0][4][:, 0:rows] + fs[1] * got[1][4][:, 0:rows]
            tangent = fs[0] * got[0][4][:, rows:] + fs[1] * got[1][4][:, rows:]
            own_part[place, head, :, 0:rows] = merged
            own_part[place, head, :, rows:] = tangent
            own_stat[place, head] = jnp.concatenate(
                [top, total, drift_total, jnp.zeros((5, rows), jnp.float32)], axis=0
            )

    def held(dest, head):
        stat = own_stat[dest, head]
        return stat[0:1], stat[1:2], stat[2:3], own_part[dest, head]

    def joined(have, way, dest, head):
        stat = stat_in[way, dest, head]
        unit = jnp.concatenate([stat[3:4], stat[4:5]], axis=1)
        part = part_in[way, dest, head].astype(jnp.int32).astype(jnp.float32) * unit
        top = jnp.maximum(have[0], stat[0:1])
        fa, fb = jnp.exp(have[0] - top), jnp.exp(stat[0:1] - top)
        return (
            top,
            fa * have[1] + fb * stat[1:2],
            fa * have[2] + fb * stat[2:3],
            jnp.concatenate([fa, fa], axis=1) * have[3]
            + jnp.concatenate([fb, fb], axis=1) * part,
        )

    def send_on(lag, way, dest, head):
        have = held(dest, head)
        if lag > 0:
            for copy in part_copies(way, dest, head):
                copy.wait_recv()
            have = joined(have, way, dest, head)
        top, total, drift_total, part = have
        unit = jnp.maximum(jnp.max(jnp.abs(part), axis=0, keepdims=True), 1e-25) / 32767.0
        coded = jnp.round(part * (1.0 / unit))
        part_out[dest, head] = coded.astype(jnp.int32).astype(jnp.int16)
        stat_out[dest, head] = jnp.concatenate(
            [
                top,
                total,
                drift_total,
                unit[:, 0:rows],
                unit[:, rows:],
                jnp.zeros((3, rows), jnp.float32),
            ],
            axis=0,
        )
        for copy in part_copies(way, dest, head):
            copy.start()

    def relay(lag, head):
        @pl.when(pos == lag)
        def _():
            for dest in range(LINE - 1, lag, -1):
                send_on(lag, 0, dest, head)

        @pl.when(pos == LINE - 1 - lag)
        def _():
            for dest in range(LINE - 1 - lag):
                send_on(lag, 1, dest, head)

    def merge(head):
        @pl.when(pos > 0)
        def _():
            for copy in part_copies(0, pos, head):
                copy.wait_recv()

        @pl.when(pos < LINE - 1)
        def _():
            for copy in part_copies(1, pos, head):
                copy.wait_recv()

        have = joined(joined(held(pos, head), 0, pos, head), 1, pos, head)
        _top, total, drift_total, part = have
        attended = part[:, 0:rows] / total
        attended_tangent = part[:, rows:] / total - drift_total / total * attended
        out_ref[:, cols(head)] = attended.T.astype(jnp.bfloat16)
        dout_ref[:, cols(head)] = attended_tangent.T.astype(jnp.bfloat16)

    def step(t, carry):
        @pl.when(t + AHEAD < heads)
        def _():
            start_kv(t + AHEAD)

        @pl.when(t + LEAD < heads)
        def _():
            start_q(t + LEAD)

        def staged(behind, run):
            @pl.when((t >= behind) & (t < heads + behind))
            def _():
                run(t - behind)

        staged(0, lambda head: forward(head, 1))
        staged(1, lambda head: forward(head, 2))
        staged(3, lambda head: relay(1, head))
        staged(4, lambda head: relay(2, head))

        def main(head):
            forward(head, 3)
            compute(head)
            relay(0, head)

        staged(2, main)
        staged(5, merge)
        return carry

    lax.fori_loop(0, heads + 5, step, 0)

    for s in shares_far:
        norm_copy(share, s).wait_send()
    for place in far:
        pick_copy(pos, place).wait_send()

    def drain(head, carry):
        kv_copy(0, head).wait_send()
        kv_copy(1, head).wait_send()
        for place in far:
            for copy in part_copies(0, place, head):
                copy.wait_send()
        for hop in range(LINE - 1):

            @pl.when((pos >= hop) & (pos < LINE - 1))
            def _():
                q_copy(pos - hop, head, 0).wait_send()

            @pl.when((pos < LINE - hop) & (pos > 0))
            def _():
                q_copy(pos + hop, head, 1).wait_send()

        return carry

    lax.fori_loop(0, heads, drain, 0)


def dense_local(query_raw, query_tangent, norm_gain, mem_keys, mem_values, retrieved):
    shares = lax.axis_size("pb")
    owners = lax.axis_size("mem")
    rows, width = query_raw.shape
    frame = mem_keys.shape[0]
    heads = width // HDIM
    named = jnp.arange(owners, dtype=jnp.int32)[:, None, None] == retrieved[None]
    picked = jnp.repeat(jnp.any(named, axis=2), QBLK, axis=1).astype(jnp.float32)
    vmem = pl.BlockSpec(memory_space=pltpu.VMEM)
    dma = pltpu.SemaphoreType.DMA
    f32, bf16 = jnp.float32, jnp.bfloat16
    return pl.pallas_call(
        functools.partial(fused_kernel, heads, shares, width * shares),
        out_shape=(jax.ShapeDtypeStruct((rows, width), bf16),) * 2,
        in_specs=[vmem] * 6,
        out_specs=(vmem, vmem),
        scratch_shapes=[
            pltpu.VMEM((2, heads, frame, HDIM), bf16),
            pltpu.VMEM((8, rows), f32),
            pltpu.VMEM((shares, 8, rows), f32),
            pltpu.VMEM((LINE, owners, rows), f32),
            pltpu.VMEM((LINE, heads, 2 * rows, HDIM), bf16),
            pltpu.VMEM((LINE, heads, HDIM, 2 * rows), jnp.int16),
            pltpu.VMEM((2, LINE, heads, HDIM, 2 * rows), jnp.int16),
            pltpu.VMEM((LINE, heads, 8, rows), f32),
            pltpu.VMEM((2, LINE, heads, 8, rows), f32),
            pltpu.VMEM((LINE, heads, HDIM, 2 * rows), f32),
            pltpu.VMEM((LINE, heads, 8, rows), f32),
            dma((2, heads)),
            dma((2, heads)),
            dma((shares,)),
            dma((shares,)),
            dma((LINE,)),
            dma((LINE,)),
            dma((LINE, 2, heads)),
            dma((LINE, heads)),
            dma((LINE, heads)),
            dma((2, LINE, heads)),
            dma((LINE, heads)),
            dma((2, LINE, heads)),
        ],
        compiler_params=pltpu.CompilerParams(
            collective_id=0, has_side_effects=True, vmem_limit_bytes=48 * 2**20
        ),
    )(query_raw, query_tangent, norm_gain.reshape(1, width), mem_keys, mem_values, picked)


def solution(mesh):
    placed = (
        P("mem", "pb"),
        P("mem", "pb"),
        P("pb"),
        P("mem", "pb"),
        P("mem", "pb"),
        P("mem", None),
    )
    dense = mesh.shape["mem"] == 2 * LINE
    return jax.shard_map(
        dense_local if dense else local,
        mesh=mesh,
        in_specs=placed,
        out_specs=(P("mem", "pb"), P("mem", "pb")),
        check_vma=False,
    )
```

```python
import functools
import math

import jax
import jax.numpy as jnp
from jax import lax
from jax.experimental import pallas as pl
from jax.experimental.pallas import tpu as pltpu
from jax.sharding import PartitionSpec as P

HEADS = 40
HDIM = 128
QBLK = 4


EPSILON = 1e-06


def head_partials(query_rows, tangent_rows, mem_keys, mem_values, head_count):
    row_count = query_rows.shape[0]
    score_scale = 1.0 / math.sqrt(HDIM)
    feature_width = head_count * HDIM
    dims_spec = (((1,), (1,)), ((), ()))

    def head_step(head_index, carry):
        start = head_index * HDIM
        query_head = lax.dynamic_slice_in_dim(query_rows, start, HDIM, 1)
        key_head = lax.dynamic_slice_in_dim(mem_keys, start, HDIM, 1)
        value_head = lax.dynamic_slice_in_dim(mem_values, start, HDIM, 1)
        scores = (
            lax.dot_general(query_head, key_head, dims_spec, preferred_element_type=jnp.float32)
            * score_scale
        )
        peak = jnp.max(scores, axis=1)
        weights = jnp.exp(scores - peak[:, None])
        updated = list(carry)
        total = jnp.sum(weights, axis=1)
        out_head = jnp.dot(
            weights.astype(jnp.bfloat16), value_head, preferred_element_type=jnp.float32
        ).astype(jnp.bfloat16)
        updated[0] = lax.dynamic_update_slice_in_dim(carry[0], out_head, start, 1)
        updated[1] = lax.dynamic_update_slice_in_dim(carry[1], peak[:, None], head_index, 1)
        updated[2] = lax.dynamic_update_slice_in_dim(carry[2], total[:, None], head_index, 1)
        tangent_head = lax.dynamic_slice_in_dim(tangent_rows, start, HDIM, 1)
        dscores = (
            lax.dot_general(tangent_head, key_head, dims_spec, preferred_element_type=jnp.float32)
            * score_scale
        )
        drift = weights * dscores
        drift_total = jnp.sum(drift, axis=1)
        tangent_out = jnp.dot(
            drift.astype(jnp.bfloat16), value_head, preferred_element_type=jnp.float32
        ).astype(jnp.bfloat16)
        updated[3] = lax.dynamic_update_slice_in_dim(carry[3], tangent_out, start, 1)
        updated[4] = lax.dynamic_update_slice_in_dim(carry[4], drift_total[:, None], head_index, 1)
        return tuple(updated)

    stat_zeros = jnp.zeros((row_count, head_count), jnp.float32)
    wide_zeros = jnp.zeros((row_count, feature_width), jnp.bfloat16)
    initial = (wide_zeros, stat_zeros, stat_zeros, wide_zeros, stat_zeros)
    return lax.fori_loop(0, head_count, head_step, initial)


def local(query_raw, query_tangent, norm_gain, mem_keys, mem_values, retrieved):
    owners = lax.axis_size("mem")
    block_count, pick_count = retrieved.shape
    token_count, feature_width = query_raw.shape
    head_count = feature_width // HDIM
    capacity = max(2, 2 * block_count * pick_count // owners)
    values_f = query_raw.astype(jnp.float32)
    tangent_f = query_tangent.astype(jnp.float32)
    square_sum, cross_sum = lax.psum(
        (jnp.sum(values_f * values_f, axis=1), jnp.sum(values_f * tangent_f, axis=1)), "pb"
    )
    full_width = HEADS * HDIM
    inverse = lax.rsqrt(square_sum / full_width + EPSILON)[:, None]
    cross_mean = (cross_sum / full_width)[:, None]
    normed = (values_f * inverse * norm_gain).astype(jnp.bfloat16)
    normed_tangent = (
        norm_gain * (tangent_f * inverse - values_f * (inverse**3 * cross_mean))
    ).astype(jnp.bfloat16)
    flat_ids = retrieved.reshape(-1)
    one_hot = (flat_ids[:, None] == jnp.arange(owners, dtype=jnp.int32)[None, :]).astype(jnp.int32)
    earlier = jnp.cumsum(one_hot, axis=0) - one_hot
    position = jnp.sum(earlier * one_hot, axis=1)
    target = flat_ids * capacity + position

    def pack(rows_in):
        copies = jnp.repeat(rows_in.reshape(block_count, QBLK, feature_width), pick_count, axis=0)
        buffer_rows = (
            jnp.zeros((owners * capacity, QBLK, feature_width), jnp.bfloat16).at[target].set(copies)
        )
        return buffer_rows.reshape(owners, capacity * QBLK, feature_width)

    send_query = pack(normed)
    send_tangent = pack(normed_tangent)

    def flatten(piece):
        return piece.reshape(-1, piece.shape[-1])

    def unflatten(array, sources, slot_rows):
        return array.reshape(sources, slot_rows, array.shape[-1])

    pieces = (
        lax.all_to_all(send_query, "mem", split_axis=0, concat_axis=0, tiled=True),
        lax.all_to_all(send_tangent, "mem", split_axis=0, concat_axis=0, tiled=True),
    )
    sources, slot_rows, _unused = pieces[0].shape
    out_part, peak_part, total_part, tangent_part, drift_part = head_partials(
        flatten(pieces[0]), flatten(pieces[1]), mem_keys, mem_values, head_count
    )
    partial_out = lax.all_to_all(
        unflatten(out_part, sources, slot_rows).astype(jnp.float32),
        "mem",
        split_axis=0,
        concat_axis=0,
        tiled=True,
    ).astype(jnp.bfloat16)
    peaks = lax.all_to_all(
        unflatten(peak_part, sources, slot_rows), "mem", split_axis=0, concat_axis=0, tiled=True
    )
    totals = lax.all_to_all(
        unflatten(total_part, sources, slot_rows), "mem", split_axis=0, concat_axis=0, tiled=True
    )
    partial_tangent = lax.all_to_all(
        unflatten(tangent_part, sources, slot_rows).astype(jnp.float32),
        "mem",
        split_axis=0,
        concat_axis=0,
        tiled=True,
    ).astype(jnp.bfloat16)
    drifts = lax.all_to_all(
        unflatten(drift_part, sources, slot_rows), "mem", split_axis=0, concat_axis=0, tiled=True
    )

    def pick_rows(array, trailing):
        slots = array.reshape((owners * capacity, QBLK) + trailing)
        return slots[target].reshape((block_count, pick_count, QBLK) + trailing)

    out_picked = pick_rows(partial_out, (head_count, HDIM))
    tangent_picked = pick_rows(partial_tangent, (head_count, HDIM))
    peak_picked = pick_rows(peaks, (head_count,))
    total_picked = pick_rows(totals, (head_count,))
    drift_picked = pick_rows(drifts, (head_count,))
    top = jnp.max(peak_picked, axis=1)
    factor = jnp.exp(peak_picked - top[:, None])
    merged_total = jnp.sum(factor * total_picked, axis=1)[..., None]
    merged_drift = jnp.sum(factor * drift_picked, axis=1)[..., None]
    merged = jnp.sum(factor[..., None] * out_picked.astype(jnp.float32), axis=1)
    merged_tangent = jnp.sum(factor[..., None] * tangent_picked.astype(jnp.float32), axis=1)
    attended = merged / merged_total
    attended_tangent = merged_tangent / merged_total - merged_drift / merged_total * attended
    return (
        attended.astype(jnp.bfloat16).reshape(token_count, feature_width),
        attended_tangent.astype(jnp.bfloat16).reshape(token_count, feature_width),
    )

LINE = 4
NEG = -1e30
AHEAD = 4
LAGS = (0, 1, 2, 4, 6, 8)
LEAD = 2
MESH = pl.DeviceIdType.MESH
NT = (((1,), (1,)), ((), ()))


def fused_kernel(
    heads,
    shares,
    full_width,
    raw_ref,
    tan_ref,
    gain_ref,
    keys_ref,
    vals_ref,
    picked_ref,
    out_ref,
    dout_ref,
    kv_in,
    norm_out,
    norm_in,
    pick_all,
    q_all,
    part_out,
    part_in,
    stat_out,
    stat_in,
    own_part,
    own_stat,
    kv_send,
    kv_recv,
    norm_send,
    norm_recv,
    pick_send,
    pick_recv,
    q_send,
    q_recv,
    part_send,
    part_recv,
    stat_send,
    stat_recv,
):
    me = lax.axis_index("mem")
    share = lax.axis_index("pb")
    pos, side = me // 2, lax.rem(me, 2)
    rows = raw_ref.shape[0]
    scale = 1.0 / math.sqrt(HDIM)

    def mem_of(position):
        return position * 2 + side

    other_side = pos * 2 + (1 - side)
    far = [lax.rem(pos + j, LINE) for j in range(1, LINE)]
    shares_far = [lax.rem(share + j, shares) for j in range(1, shares)]

    def cols(head):
        return pl.ds(pl.multiple_of(head * HDIM, HDIM), HDIM)

    barrier = pltpu.get_barrier_semaphore()
    pl.semaphore_signal(
        barrier, inc=1, device_id={"mem": other_side, "pb": share}, device_id_type=MESH
    )
    for place in far:
        pl.semaphore_signal(
            barrier, inc=1, device_id={"mem": mem_of(place), "pb": share}, device_id_type=MESH
        )
    for s in shares_far:
        pl.semaphore_signal(barrier, inc=1, device_id={"mem": me, "pb": s}, device_id_type=MESH)
    pl.semaphore_wait(barrier, 1 + len(far) + len(shares_far))

    def remote(src, dst, send, recv, mem, pb):
        return pltpu.make_async_remote_copy(
            src_ref=src,
            dst_ref=dst,
            send_sem=send,
            recv_sem=recv,
            device_id={"mem": mem, "pb": pb},
            device_id_type=MESH,
        )

    def kv_copy(which, head):
        src = (keys_ref, vals_ref)[which].at[:, cols(head)]
        return remote(
            src,
            kv_in.at[which, head],
            kv_send.at[which, head],
            kv_recv.at[which, head],
            other_side,
            share,
        )

    def norm_copy(slot, to):
        return remote(
            norm_out, norm_in.at[slot], norm_send.at[to], norm_recv.at[slot], me, to
        )

    def pick_copy(slot, to):
        return remote(
            picked_ref,
            pick_all.at[slot],
            pick_send.at[to],
            pick_recv.at[slot],
            mem_of(to),
            share,
        )

    def q_copy(origin, head, way):
        to = lax.rem(pos + (1 if way == 0 else LINE - 1), LINE)
        return remote(
            q_all.at[origin, head],
            q_all.at[origin, head],
            q_send.at[origin, way, head],
            q_recv.at[origin, head],
            mem_of(to),
            share,
        )

    def part_copies(way, dest, head):
        to = mem_of(lax.rem(pos + (1 if way == 0 else LINE - 1), LINE))
        return (
            remote(
                part_out.at[dest, head],
                part_in.at[way, dest, head],
                part_send.at[dest, head],
                part_recv.at[way, dest, head],
                to,
                share,
            ),
            remote(
                stat_out.at[dest, head],
                stat_in.at[way, dest, head],
                stat_send.at[dest, head],
                stat_recv.at[way, dest, head],
                to,
                share,
            ),
        )

    def add_sums(head, carry):
        square, cross = carry
        raw = raw_ref[:, cols(head)].astype(jnp.float32)
        tan = tan_ref[:, cols(head)].astype(jnp.float32)
        return square + raw * raw, cross + raw * tan

    blank = jnp.zeros((rows, HDIM), jnp.float32)
    square, cross = lax.fori_loop(0, heads, add_sums, (blank, blank))
    lane = lax.broadcasted_iota(jnp.int32, (rows, HDIM), 1)
    sums = jnp.where(
        lane == 0,
        jnp.sum(square, axis=1, keepdims=True),
        jnp.where(lane == 1, jnp.sum(cross, axis=1, keepdims=True), 0.0),
    )
    sums_t = sums.T[0:8, :]
    norm_out[...] = sums_t
    for s in shares_far:
        norm_copy(share, s).start()
    for place in far:
        pick_copy(pos, place).start()

    def start_kv(head):
        kv_copy(0, head).start()
        kv_copy(1, head).start()

    stat_row0 = jnp.where(
        lax.broadcasted_iota(jnp.int32, (heads, 8, rows), 1) == 0, 1.0, 0.0
    )
    for head in range(min(AHEAD, heads)):
        start_kv(head)

    @pl.when(pos == 0)
    def _():
        part_in[0, 0] = jnp.zeros_like(part_in[0, 0])
        stat_in[0, 0] = jnp.full_like(stat_in[0, 0], NEG) * stat_row0

    @pl.when(pos == LINE - 1)
    def _():
        part_in[1, LINE - 1] = jnp.zeros_like(part_in[1, LINE - 1])
        stat_in[1, LINE - 1] = jnp.full_like(stat_in[1, LINE - 1], NEG) * stat_row0

    for s in shares_far:
        norm_copy(s, s).wait_recv()
        sums_t = sums_t + norm_in[s]
    sums = jnp.concatenate([sums_t] + [jnp.zeros_like(sums_t)] * (HDIM // 8 - 1), axis=0).T
    inverse = lax.rsqrt(sums[:, 0:1] / full_width + EPSILON)
    cross_mean = sums[:, 1:2] / full_width
    slope = inverse**3 * cross_mean

    def normalize(head, carry):
        raw = raw_ref[:, cols(head)].astype(jnp.float32)
        tan = tan_ref[:, cols(head)].astype(jnp.float32)
        gain = gain_ref[:, cols(head)]
        q_all[pos, head, 0:rows, :] = (raw * inverse * gain).astype(jnp.bfloat16)
        q_all[pos, head, rows : 2 * rows, :] = (gain * (tan * inverse - raw * slope)).astype(
            jnp.bfloat16
        )
        return carry

    def start_q(head):
        @pl.when(pos < LINE - 1)
        def _():
            q_copy(pos, head, 0).start()

        @pl.when(pos > 0)
        def _():
            q_copy(pos, head, 1).start()

    for head in range(min(LEAD, heads)):
        normalize(head, 0)
        start_q(head)
    lax.fori_loop(min(LEAD, heads), heads, normalize, 0)

    for place in far:
        pick_copy(place, place).wait_recv()

    def forward(head, hop):
        @pl.when(pos >= hop)
        def _():
            q_copy(pos - hop, head, 0).wait_recv()

            @pl.when(pos < LINE - 1)
            def _():
                q_copy(pos - hop, head, 0).start()

        @pl.when(pos < LINE - hop)
        def _():
            q_copy(pos + hop, head, 1).wait_recv()

            @pl.when(pos > 0)
            def _():
                q_copy(pos + hop, head, 1).start()

    frame_row = lax.broadcasted_iota(jnp.int32, (8, rows), 0)

    def compute(head):
        kv_copy(0, head).wait_recv()
        kv_copy(1, head).wait_recv()
        frames = (
            (me, keys_ref[:, cols(head)], vals_ref[:, cols(head)].T),
            (other_side, kv_in[0, head], kv_in[1, head].T),
        )
        for place in far + [pos]:
            query = q_all[place, head]
            masks = picked_ref[...] if place is pos else pick_all[place]
            got = []
            for frame, keys, vals_t in frames:
                both = lax.dot_general(keys, query, NT, preferred_element_type=jnp.float32) * scale
                score, dscore = both[:, 0:rows], both[:, rows : 2 * rows]
                peak = jnp.max(score, axis=0, keepdims=True)
                weight = jnp.exp(score - peak)
                drift = weight * dscore
                mixed = jnp.concatenate(
                    [weight.astype(jnp.bfloat16), drift.astype(jnp.bfloat16)], axis=1
                )
                part = jnp.dot(vals_t, mixed, preferred_element_type=jnp.float32)
                mask = jnp.sum(jnp.where(frame_row == frame, masks, 0.0), axis=0, keepdims=True)
                got.append(
                    (
                        mask,
                        jnp.where(mask > 0.0, peak, NEG),
                        jnp.sum(weight, axis=0, keepdims=True),
                        jnp.sum(drift, axis=0, keepdims=True),
                        part.astype(jnp.bfloat16).astype(jnp.float32),
                    )
                )
            top = jnp.maximum(got[0][1], got[1][1])
            fs = [jnp.exp(g[1] - top) * g[0] for g in got]
            total = fs[0] * got[0][2] + fs[1] * got[1][2]
            drift_total = fs[0] * got[0][3] + fs[1] * got[1][3]
            merged = fs[0] * got[0][4][:, 0:rows] + fs[1] * got[1][4][:, 0:rows]
            tangent = fs[0] * got[0][4][:, rows:] + fs[1] * got[1][4][:, rows:]
            own_part[place, head, :, 0:rows] = merged
            own_part[place, head, :, rows:] = tangent
            own_stat[place, head] = jnp.concatenate(
                [top, total, drift_total, jnp.zeros((5, rows), jnp.float32)], axis=0
            )

    def held(dest, head):
        stat = own_stat[dest, head]
        return stat[0:1], stat[1:2], stat[2:3], own_part[dest, head]

    def joined(have, way, dest, head):
        stat = stat_in[way, dest, head]
        unit = jnp.concatenate([stat[3:4], stat[4:5]], axis=1)
        part = part_in[way, dest, head].astype(jnp.int32).astype(jnp.float32) * unit
        top = jnp.maximum(have[0], stat[0:1])
        fa, fb = jnp.exp(have[0] - top), jnp.exp(stat[0:1] - top)
        return (
            top,
            fa * have[1] + fb * stat[1:2],
            fa * have[2] + fb * stat[2:3],
            jnp.concatenate([fa, fa], axis=1) * have[3]
            + jnp.concatenate([fb, fb], axis=1) * part,
        )

    def send_on(lag, way, dest, head):
        have = held(dest, head)
        if lag > 0:
            for copy in part_copies(way, dest, head):
                copy.wait_recv()
            have = joined(have, way, dest, head)
        top, total, drift_total, part = have
        unit = jnp.maximum(jnp.max(jnp.abs(part), axis=0, keepdims=True), 1e-25) / 32767.0
        coded = jnp.round(part * (1.0 / unit))
        part_out[dest, head] = coded.astype(jnp.int32).astype(jnp.int16)
        stat_out[dest, head] = jnp.concatenate(
            [
                top,
                total,
                drift_total,
                unit[:, 0:rows],
                unit[:, rows:],
                jnp.zeros((3, rows), jnp.float32),
            ],
            axis=0,
        )
        for copy in part_copies(way, dest, head):
            copy.start()

    def relay(lag, head):
        @pl.when(pos == lag)
        def _():
            for dest in range(LINE - 1, lag, -1):
                send_on(lag, 0, dest, head)

        @pl.when(pos == LINE - 1 - lag)
        def _():
            for dest in range(LINE - 1 - lag):
                send_on(lag, 1, dest, head)

    def merge(head):
        @pl.when(pos > 0)
        def _():
            for copy in part_copies(0, pos, head):
                copy.wait_recv()

        @pl.when(pos < LINE - 1)
        def _():
            for copy in part_copies(1, pos, head):
                copy.wait_recv()

        have = joined(joined(held(pos, head), 0, pos, head), 1, pos, head)
        _top, total, drift_total, part = have
        attended = part[:, 0:rows] / total
        attended_tangent = part[:, rows:] / total - drift_total / total * attended
        out_ref[:, cols(head)] = attended.T.astype(jnp.bfloat16)
        dout_ref[:, cols(head)] = attended_tangent.T.astype(jnp.bfloat16)

    def step(t, carry):
        @pl.when(t + AHEAD < heads)
        def _():
            start_kv(t + AHEAD)

        @pl.when(t + LEAD < heads)
        def _():
            start_q(t + LEAD)

        def staged(behind, run):
            @pl.when((t >= behind) & (t < heads + behind))
            def _():
                run(t - behind)

        staged(LAGS[0], lambda head: forward(head, 1))
        staged(LAGS[1], lambda head: forward(head, 2))
        staged(LAGS[3], lambda head: relay(1, head))
        staged(LAGS[4], lambda head: relay(2, head))

        def main(head):
            forward(head, 3)
            compute(head)
            relay(0, head)

        staged(LAGS[2], main)
        staged(LAGS[5], merge)
        return carry

    lax.fori_loop(0, heads + LAGS[5], step, 0)

    for s in shares_far:
        norm_copy(share, s).wait_send()
    for place in far:
        pick_copy(pos, place).wait_send()

    def drain(head, carry):
        kv_copy(0, head).wait_send()
        kv_copy(1, head).wait_send()
        for place in far:
            for copy in part_copies(0, place, head):
                copy.wait_send()
        for hop in range(LINE - 1):

            @pl.when((pos >= hop) & (pos < LINE - 1))
            def _():
                q_copy(pos - hop, head, 0).wait_send()

            @pl.when((pos < LINE - hop) & (pos > 0))
            def _():
                q_copy(pos + hop, head, 1).wait_send()

        return carry

    lax.fori_loop(0, heads, drain, 0)


def dense_local(query_raw, query_tangent, norm_gain, mem_keys, mem_values, retrieved):
    shares = lax.axis_size("pb")
    owners = lax.axis_size("mem")
    rows, width = query_raw.shape
    frame = mem_keys.shape[0]
    heads = width // HDIM
    named = jnp.arange(owners, dtype=jnp.int32)[:, None, None] == retrieved[None]
    picked = jnp.repeat(jnp.any(named, axis=2), QBLK, axis=1).astype(jnp.float32)
    vmem = pl.BlockSpec(memory_space=pltpu.VMEM)
    dma = pltpu.SemaphoreType.DMA
    f32, bf16 = jnp.float32, jnp.bfloat16
    return pl.pallas_call(
        functools.partial(fused_kernel, heads, shares, width * shares),
        out_shape=(jax.ShapeDtypeStruct((rows, width), bf16),) * 2,
        in_specs=[vmem] * 6,
        out_specs=(vmem, vmem),
        scratch_shapes=[
            pltpu.VMEM((2, heads, frame, HDIM), bf16),
            pltpu.VMEM((8, rows), f32),
            pltpu.VMEM((shares, 8, rows), f32),
            pltpu.VMEM((LINE, owners, rows), f32),
            pltpu.VMEM((LINE, heads, 2 * rows, HDIM), bf16),
            pltpu.VMEM((LINE, heads, HDIM, 2 * rows), jnp.int16),
            pltpu.VMEM((2, LINE, heads, HDIM, 2 * rows), jnp.int16),
            pltpu.VMEM((LINE, heads, 8, rows), f32),
            pltpu.VMEM((2, LINE, heads, 8, rows), f32),
            pltpu.VMEM((LINE, heads, HDIM, 2 * rows), f32),
            pltpu.VMEM((LINE, heads, 8, rows), f32),
            dma((2, heads)),
            dma((2, heads)),
            dma((shares,)),
            dma((shares,)),
            dma((LINE,)),
            dma((LINE,)),
            dma((LINE, 2, heads)),
            dma((LINE, heads)),
            dma((LINE, heads)),
            dma((2, LINE, heads)),
            dma((LINE, heads)),
            dma((2, LINE, heads)),
        ],
        compiler_params=pltpu.CompilerParams(
            collective_id=0, has_side_effects=True, vmem_limit_bytes=48 * 2**20
        ),
    )(query_raw, query_tangent, norm_gain.reshape(1, width), mem_keys, mem_values, picked)


def solution(mesh):
    placed = (
        P("mem", "pb"),
        P("mem", "pb"),
        P("pb"),
        P("mem", "pb"),
        P("mem", "pb"),
        P("mem", None),
    )
    dense = mesh.shape["mem"] == 2 * LINE
    return jax.shard_map(
        dense_local if dense else local,
        mesh=mesh,
        in_specs=placed,
        out_specs=(P("mem", "pb"), P("mem", "pb")),
        check_vma=False,
    )
```
